128 devices in a mesh: dp: 64 (over z, y, x_lo, core), mp: 2 (over x_hi).
Axes of the slice: x: 4 (x_hi: 2, x_lo: 2; x = x_hi * 2 + x_lo), y: 4, z: 4, core: 2. Of those that a mesh axis runs over, the one named last changes fastest.
Arguments:
- grad_parts: bfloat16 [64, 1, 7168, 1024], P('dp', None, 'mp'), may hold values from -850.5 to 850.5
- master: float32 [1, 2, 3584, 1024], P(None, 'mp', 'dp'), may hold values from -3 to 3
- momentum: float32 [1, 2, 3584, 1024], P(None, 'mp', 'dp'), may hold values from -1.5 to 1.5
Outputs:
- new_weights: bfloat16 [1, 7168, 1024], P(None, 'mp')
- new_momentum: float32 [1, 2, 3584, 1024], P(None, 'mp', 'dp')
- new_master: float32 [1, 2, 3584, 1024], P(None, 'mp', 'dp')
- update: float32 [1, 2, 3584, 1024], P(None, 'mp', 'dp')
The draws below stay inside these ranges and needn't reach their ends.
All inputs are finite; a program needn't handle non-finite values.
Results may differ from the reference program's by a relative error of at most 0.001.
Values may be sent and summed in bfloat16 or wider, within the bound.
No kernel may reach another device: no remote copies, remote signals or barrier semaphores. Data moves between devices by JAX's collectives and lax.ppermute only.
A program may use at most 128 MiB of HBM per device.

```python
import jax
import jax.numpy as jnp
from jax import lax

D = 7168
H = 1024
EXPERTS = 1
ITERS = 3
N_DP = 64
N_MP = 2


def log_spread(key, shape, lower, upper):
    return jnp.exp(jax.random.uniform(key, shape, jnp.float32, jnp.log(lower), jnp.log(upper)))


def draw_grad_parts(key, part):
    key = jax.random.fold_in(key, 11)
    keys = jax.random.split(key, 5)
    shape = (N_DP, EXPERTS, D, H)
    noise = jax.random.truncated_normal(keys[1], -6.0, 6.0, shape, jnp.float32)
    rise = 2.0
    replica = 1.0 + 2.0 * jnp.arange(N_DP, dtype=jnp.float32) / max(N_DP - 1, 1)
    row_rise = 1.0 + rise * jnp.arange(D, dtype=jnp.float32) / D
    row_scale = row_rise[None, :] * log_spread(keys[2], (EXPERTS, D), 1.0, 3.5)
    col_scale = log_spread(keys[3], (EXPERTS, H), 1.0, 30.0)
    block_count = N_DP * N_MP
    block_rows = D // block_count
    owner = jax.random.permutation(keys[4], block_count).astype(jnp.int32)
    block_index = jnp.arange(D, dtype=jnp.int32) // block_rows
    target = owner[block_index] % H
    column_key = jnp.arange(H, dtype=jnp.int32) % block_count
    heavy = jnp.where(target[:, None] == column_key[None, :], 12.0, 1.0)
    value = noise * replica[:, None, None, None] * row_scale[None, :, :, None] * col_scale[None, :, None, :] * heavy[None, None, :, :]
    value = value / (20.0 * N_DP ** 0.5)
    return value.astype(jnp.bfloat16)


def block_levels(stream_key, shape, cuts, low, largest):
    factor_of = 1.0
    for position, parts in cuts:
        heights = jax.random.uniform(jax.random.fold_in(jax.random.fold_in(stream_key, 6), position), (parts,), jnp.float32, low / len(cuts), largest / len(cuts))
        factor_of = factor_of * jnp.repeat(jnp.exp(heights), shape[position] // parts).reshape((-1,) + (1,) * (len(shape) - 1 - position))
    return factor_of


def scatter_about(rng, extent, deviation, bound, shards=(), kind=jnp.bfloat16):
    values = jax.random.normal(rng, extent, jnp.float32) * deviation
    if len(shards) > 0:
        values = block_levels(rng, extent, shards, -0.22, 0.18) * values
    return jnp.clip(values, min=-bound, max=bound).astype(kind)


def setup_inputs(seed: int = 0) -> dict:
    seeds = jax.random.split(jax.random.key(seed), 4)
    grad_parts = draw_grad_parts(jax.random.fold_in(seeds[3], 71), 0)
    master = scatter_about(seeds[1], (EXPERTS, N_MP, D // N_MP, H), 0.5, 3.0, ((1, 2), (2, 64)), jnp.float32)
    momentum = scatter_about(seeds[2], (EXPERTS, N_MP, D // N_MP, H), 0.25, 1.5, ((1, 2), (2, 64)), jnp.float32)
    return {"grad_parts": grad_parts, "master": master, "momentum": momentum}


beta_rate = 0.95
learn_rate = 0.02
decay_rate = 0.1
small_eps = 1e-07
coef_first = 3.4445
coef_second = -4.775
coef_third = 2.0315

def add_part(total, piece):
    return (total + piece.astype(jnp.float32), None)

def reference(grad_parts, master, momentum):
    summed_grad, _ = lax.scan(add_part, jnp.zeros(grad_parts.shape[1:], jnp.float32), grad_parts)
    count = master.shape[0]
    old_master = master.reshape(count, D, H)
    old_momentum = momentum.reshape(count, D, H)
    new_momentum = beta_rate * old_momentum + summed_grad
    direction = summed_grad + beta_rate * new_momentum
    norms = jnp.sqrt(lax.optimization_barrier(jnp.sum(direction * direction, axis=(1, 2))))
    scaled = direction / (norms + small_eps)[:, None, None]
    for step in range(ITERS):
        gram = jnp.einsum('erh,erk->ehk', scaled, scaled, precision=lax.Precision.HIGHEST)
        square = jnp.einsum('ehk,ekl->ehl', gram, gram, precision=lax.Precision.HIGHEST)
        mixed = coef_second * gram + coef_third * square
        scaled = coef_first * scaled + jnp.einsum('erh,ehk->erk', scaled, mixed, precision=lax.Precision.HIGHEST)
    factor = 0.2 * max(D, H) ** 0.5
    update = factor * scaled
    new_master = old_master * (1.0 - learn_rate * decay_rate) - learn_rate * update
    new_weights = new_master.astype(jnp.bfloat16)
    return (new_weights, new_momentum.reshape(momentum.shape), new_master.reshape(master.shape), update.reshape(master.shape))
```

```python
import jax
import jax.numpy as jnp
import numpy as np
from jax import lax
from jax.experimental import pallas as pl
from jax.experimental.pallas import tpu as pltpu
from jax.sharding import Mesh, PartitionSpec as P

D = 7168
H = 1024
ITERS = 3
N_DP = 64
ROWS = 56
BLOCK = 256
UPPER = [(i, j) for i in range(H // BLOCK) for j in range(i, H // BLOCK)]
PACKED = len(UPPER) * BLOCK * BLOCK // 128

beta_rate = 0.95
learn_rate = 0.02
decay_rate = 0.1
small_eps = 1e-07
coef_first = 3.4445
coef_second = -4.775
coef_third = 2.0315

f32 = jnp.float32
bf16 = jnp.bfloat16
CHIPS = ("z", "y", "xl", "xh")
DP = ("z", "y", "xl", "c")


def split(x):
    hi = x.astype(bf16)
    return hi, (x - hi.astype(f32)).astype(bf16)


def dot(a, b):
    return jnp.dot(a, b, preferred_element_type=f32)


STEP = 8


def gram_kernel(parts, momentum, new_momentum, direction, gram, total):
    step = pl.program_id(0)
    piece = parts[0].astype(f32)
    for i in range(1, STEP):
        piece += parts[i].astype(f32)

    @pl.when(step == 0)
    def _():
        total[...] = piece

    @pl.when(step > 0)
    def _():
        total[...] += piece

    @pl.when(step == N_DP // STEP - 1)
    def _():
        grad = total[...]
        moved = beta_rate * momentum[...] + grad
        new_momentum[...] = moved
        direct = grad + beta_rate * moved
        direction[...] = direct
        hi, lo = split(direct)
        left = jnp.concatenate([hi, lo, hi, lo], axis=0).T
        right = jnp.concatenate([hi, hi, lo, lo], axis=0)
        place = 0
        for i in range(H // BLOCK):
            wide = dot(left[i * BLOCK : (i + 1) * BLOCK], right[:, i * BLOCK :])
            for j in range((H // BLOCK - i) * BLOCK // 128):
                gram[pl.ds(place, BLOCK), :] = wide[:, j * 128 : (j + 1) * 128]
                place += BLOCK


def sum_and_gram(parts, momentum):
    row = pl.BlockSpec((ROWS, H), lambda i: (0, 0))
    return pl.pallas_call(
        gram_kernel,
        grid=(N_DP // STEP,),
        in_specs=[pl.BlockSpec((STEP, ROWS, H), lambda i: (i, 0, 0)), row],
        out_specs=[row, row, pl.BlockSpec((PACKED, 128), lambda i: (0, 0))],
        out_shape=[
            jax.ShapeDtypeStruct((ROWS, H), f32),
            jax.ShapeDtypeStruct((ROWS, H), f32),
            jax.ShapeDtypeStruct((PACKED, 128), f32),
        ],
        scratch_shapes=[pltpu.VMEM((ROWS, H), f32)],
        compiler_params=pltpu.CompilerParams(vmem_limit_bytes=40 * 2**20),
        name="sum_and_gram",
    )(parts, momentum)


def newton_kernel(packed, direction, master, update, new_master, weights, gram, g_hi, g_lo, p_hi, p_lo):
    n = H // BLOCK
    place = 0
    for i in range(n):
        for j in range(i, n):
            tile = jnp.concatenate(
                [packed[pl.ds(place, BLOCK), :], packed[pl.ds(place + BLOCK, BLOCK), :]], axis=1
            )
            place += 2 * BLOCK
            gram[i * BLOCK : (i + 1) * BLOCK, j * BLOCK : (j + 1) * BLOCK] = tile
            if j > i:
                gram[j * BLOCK : (j + 1) * BLOCK, i * BLOCK : (i + 1) * BLOCK] = tile.T
    rows = lax.broadcasted_iota(jnp.int32, (BLOCK, BLOCK), 0)
    cols = lax.broadcasted_iota(jnp.int32, (BLOCK, BLOCK), 1)
    on = rows == cols
    trace = jnp.zeros((), f32)
    for i in range(n):
        span = slice(i * BLOCK, (i + 1) * BLOCK)
        trace += jnp.sum(jnp.where(on, gram[span, span], 0.0))
    inverse = 1.0 / (jnp.sqrt(jnp.full((1, 1), trace, f32)) + small_eps)

    def full(a_hi, a_lo, b_hi, b_lo, span):
        b = b_hi[...]
        return dot(a_hi[span, :], b) + dot(a_lo[span, :], b) + dot(a_hi[span, :], b_lo[...])

    def thin(x, b_hi, b_lo):
        hi, lo = split(x)
        both = dot(jnp.concatenate([hi, lo], axis=0), b_hi[...])
        return both[:ROWS] + both[ROWS:] + dot(hi, b_lo[...])

    spans = [slice(i * BLOCK, (i + 1) * BLOCK) for i in range(n)]
    wide_rows = lax.broadcasted_iota(jnp.int32, (BLOCK, H), 0)
    wide_cols = lax.broadcasted_iota(jnp.int32, (BLOCK, H), 1)

    def store(value, hi_ref, lo_ref, span):
        hi, lo = split(value)
        hi_ref[span, :] = hi
        lo_ref[span, :] = lo

    for span in spans:
        value = gram[span, :] * inverse * inverse
        gram[span, :] = value
        store(value, g_hi, g_lo, span)
    scaled = direction[...] * inverse
    for step in range(ITERS):
        if step == ITERS - 1:
            first = thin(scaled, g_hi, g_lo)
            second = thin(first, g_hi, g_lo)
            scaled = coef_first * scaled + coef_second * first + coef_third * second
            break
        for i, span in enumerate(spans):
            square = full(g_hi, g_lo, g_hi, g_lo, span)
            poly = coef_second * gram[span, :] + coef_third * square
            poly += jnp.where(wide_rows + i * BLOCK == wide_cols, coef_first, 0.0)
            store(poly, p_hi, p_lo, span)
        scaled = thin(scaled, p_hi, p_lo)
        for span in spans:
            gram[span, :] = full(g_hi, g_lo, p_hi, p_lo, span)
        for span in spans:
            store(gram[span, :], g_hi, g_lo, span)
        for span in spans:
            gram[span, :] = full(g_hi, g_lo, p_hi, p_lo, span)
        for span in spans:
            store(gram[span, :], g_hi, g_lo, span)
    result = (0.2 * max(D, H) ** 0.5) * scaled
    update[...] = result
    moved = master[...] * (1.0 - learn_rate * decay_rate) - learn_rate * result
    new_master[...] = moved
    weights[...] = moved.astype(bf16)


def newton(packed, direction, master):
    whole = pl.BlockSpec(memory_space=pltpu.VMEM)
    return pl.pallas_call(
        newton_kernel,
        in_specs=[whole] * 3,
        out_specs=[whole] * 3,
        out_shape=[
            jax.ShapeDtypeStruct((ROWS, H), f32),
            jax.ShapeDtypeStruct((ROWS, H), f32),
            jax.ShapeDtypeStruct((ROWS, H), bf16),
        ],
        scratch_shapes=[pltpu.VMEM((H, H), f32)] + [pltpu.VMEM((H, H), bf16)] * 4,
        compiler_params=pltpu.CompilerParams(vmem_limit_bytes=56 * 2**20),
        name="newton",
    )(packed, direction, master)


def exchange(x, axes):
    return lax.all_to_all(x, axes, 0, 0, tiled=True)


def swap(x, axis):
    return lax.ppermute(x, axis, [(0, 1), (1, 0)])


def repeat(x, n):
    return jnp.broadcast_to(x[None], (n,) + x.shape)


def summed_gram(gram):
    core = lax.axis_index("c")
    half = PACKED // 2
    given = lax.dynamic_slice(gram, ((1 - core) * half, 0), (half, 128))
    kept = lax.dynamic_slice(gram, (core * half, 0), (half, 128))
    part = kept + swap(given, "c")
    piece = exchange(part.reshape(64, half // 64, 128), CHIPS).sum(0)
    mine = exchange(repeat(piece, 64), CHIPS).reshape(half, 128)
    other = swap(mine, "c")
    return jnp.concatenate([jnp.where(core == 0, mine, other), jnp.where(core == 0, other, mine)], 0)


def gathered(rows):
    core = lax.axis_index("c")
    low = lax.axis_index("xl") == 0
    other = swap(rows, "xl")
    pair = jnp.where(low, jnp.stack([rows, other]), jnp.stack([other, rows]))
    mine = exchange(repeat(pair, 16), ("z", "y"))
    other = swap(mine, "c")
    whole = jnp.where(core == 0, jnp.stack([mine, other], 2), jnp.stack([other, mine], 2))
    return whole.reshape(1, N_DP * ROWS, H)


def shards(grad_parts, master, momentum):
    parts = exchange(grad_parts.reshape(N_DP, ROWS, H), DP)
    new_momentum, direction, gram = sum_and_gram(parts, momentum.reshape(ROWS, H))
    update, new_master, weights = newton(summed_gram(gram), direction, master.reshape(ROWS, H))
    return (
        gathered(weights),
        new_momentum.reshape(momentum.shape),
        new_master.reshape(master.shape),
        update.reshape(master.shape),
    )


def solution(mesh):
    fine = Mesh(mesh.devices.reshape(4, 4, 2, 2, 2), ("z", "y", "xl", "c", "xh"))
    rows = P(None, "xh", DP, None)
    return jax.shard_map(
        shards,
        mesh=fine,
        in_specs=(P(DP, None, "xh", None), rows, rows),
        out_specs=(P(None, "xh", None), rows, rows, rows),
        check_vma=False,
    )
```

```python
import functools

import jax
import jax.numpy as jnp
import numpy as np
from jax import lax
from jax.experimental import pallas as pl
from jax.experimental.pallas import tpu as pltpu
from jax.sharding import Mesh, PartitionSpec as P

D = 7168
H = 1024
ITERS = 3
N_DP = 64
ROWS = 56
BLOCK = 256
UPPER = [(i, j) for i in range(H // BLOCK) for j in range(i, H // BLOCK)]
PACKED = len(UPPER) * BLOCK * BLOCK // 128

beta_rate = 0.95
learn_rate = 0.02
decay_rate = 0.1
small_eps = 1e-07
coef_first = 3.4445
coef_second = -4.775
coef_third = 2.0315

f32 = jnp.float32
bf16 = jnp.bfloat16
CHIPS = ("z", "y", "xl", "xh")
DP = ("z", "y", "xl", "c")


def split(x):
    hi = x.astype(bf16)
    return hi, (x - hi.astype(f32)).astype(bf16)


def dot(a, b):
    return jnp.dot(a, b, preferred_element_type=f32)


WIDE = H // 2


def gram_kernel(place_ref, early, late, late_other, momentum, new_momentum, direction, kept, given):
    left = early[0]
    for i in range(1, early.shape[0]):
        left += early[i]
    grad = jnp.concatenate([left, late[...] + late_other[...]], axis=1)
    moved = beta_rate * momentum[...] + grad
    new_momentum[...] = moved
    direct = grad + beta_rate * moved
    direction[...] = direct
    hi, lo = split(direct)
    tall = jnp.concatenate([hi, lo, hi, lo], axis=0).T
    deep = jnp.concatenate([hi, hi, lo, lo], axis=0)
    place = 0
    for i in range(H // BLOCK):
        wide = dot(tall[i * BLOCK : (i + 1) * BLOCK], deep[:, i * BLOCK :])
        for j in range((H // BLOCK - i) * BLOCK // 128):
            half, at = divmod(place, PACKED // 2)
            value = wide[:, j * 128 : (j + 1) * 128]

            @pl.when(place_ref[1] == half)
            def _():
                kept[pl.ds(at, BLOCK), :] = value

            @pl.when(place_ref[1] != half)
            def _():
                given[pl.ds(at, BLOCK), :] = value

            place += BLOCK


def direction_and_gram(place, early, late, late_other, momentum):
    whole = pl.BlockSpec(memory_space=pltpu.VMEM)
    row = jax.ShapeDtypeStruct((ROWS, H), f32)
    half = jax.ShapeDtypeStruct((PACKED // 2, 128), f32)
    return pl.pallas_call(
        gram_kernel,
        in_specs=[pl.BlockSpec(memory_space=pltpu.SMEM)] + [whole] * 4,
        out_specs=[whole] * 4,
        out_shape=[row, row, half, half],
        compiler_params=pltpu.CompilerParams(vmem_limit_bytes=24 * 2**20),
        name="direction_and_gram",
    )(place, early, late, late_other, momentum)


def newton_kernel(
    place_ref, mine, other, direction, direction_other, master, master_other,
    update, new_master, pairs, gram, g_hi, g_lo, p_hi, p_lo,
):
    n = H // BLOCK
    spans = [slice(i * BLOCK, (i + 1) * BLOCK) for i in range(n)]
    on = lax.broadcasted_iota(jnp.int32, (BLOCK, BLOCK), 0) == lax.broadcasted_iota(
        jnp.int32, (BLOCK, BLOCK), 1
    )
    first_core = place_ref[1] == 0

    def loaded(place):
        half, at = divmod(place, PACKED // 2)
        a, b = mine[pl.ds(at, BLOCK), :], other[pl.ds(at, BLOCK), :]
        return jnp.where(first_core, a, b) if half == 0 else jnp.where(first_core, b, a)

    def put(value, i, j, hi_ref, lo_ref):
        hi, lo = split(value)
        hi_ref[spans[i], spans[j]] = hi
        lo_ref[spans[i], spans[j]] = lo
        if j > i:
            hi_ref[spans[j], spans[i]] = hi.T
            lo_ref[spans[j], spans[i]] = lo.T

    def full(a_hi, a_lo, b_hi, b_lo, i):
        cols = slice(i * BLOCK, H)
        b = b_hi[:, cols]
        return (
            dot(a_hi[spans[i], :], b)
            + dot(a_lo[spans[i], :], b)
            + dot(a_hi[spans[i], :], b_lo[:, cols])
        )

    def thin(x, b_hi, b_lo):
        hi, lo = split(x)
        both = dot(jnp.concatenate([hi, lo], axis=0), b_hi[...])
        return both[: 2 * ROWS] + both[2 * ROWS :] + dot(hi, b_lo[...])

    def poly():
        for i in range(n):
            square = full(g_hi, g_lo, g_hi, g_lo, i)
            for j in range(i, n):
                value = coef_second * gram[spans[i], spans[j]]
                value += coef_third * square[:, (j - i) * BLOCK : (j - i + 1) * BLOCK]
                if i == j:
                    value += jnp.where(on, coef_first, 0.0)
                put(value, i, j, p_hi, p_lo)

    def times_poly():
        for i in range(n):
            gram[spans[i], i * BLOCK :] = full(g_hi, g_lo, p_hi, p_lo, i)
        for i in range(n):
            for j in range(i, n):
                put(gram[spans[i], spans[j]], i, j, g_hi, g_lo)

    place = 0
    trace = jnp.zeros((), f32)
    for i in range(n):
        for j in range(i, n):
            tile = jnp.concatenate([loaded(place), loaded(place + BLOCK)], axis=1)
            place += 2 * BLOCK
            gram[spans[i], spans[j]] = tile
            if i == j:
                trace += jnp.sum(jnp.where(on, tile, 0.0))
    inverse = 1.0 / (jnp.sqrt(jnp.full((1, 1), trace, f32)) + small_eps)
    for i in range(n):
        for j in range(i, n):
            value = gram[spans[i], spans[j]] * inverse * inverse
            gram[spans[i], spans[j]] = value
            put(value, i, j, g_hi, g_lo)

    scaled = jnp.concatenate([direction[...], direction_other[...]], axis=0) * inverse
    poly()
    scaled = thin(scaled, p_hi, p_lo)
    times_poly()
    times_poly()
    poly()
    scaled = thin(scaled, p_hi, p_lo)

    def last_gram(x):
        return thin(thin(thin(x, p_hi, p_lo), p_hi, p_lo), g_hi, g_lo)

    once = last_gram(scaled)
    twice = last_gram(once)
    scaled = coef_first * scaled + coef_second * once + coef_third * twice
    result = (0.2 * max(D, H) ** 0.5) * scaled
    update[...] = result[:ROWS]

    def stepped(old, change):
        return old * (1.0 - learn_rate * decay_rate) - learn_rate * change

    moved = stepped(master[...], result[:ROWS])
    new_master[...] = moved
    weights = moved.astype(bf16)
    weights_other = stepped(master_other[...], result[ROWS:]).astype(bf16)
    low = place_ref[0]
    for i in range(16):
        pairs[i, low] = weights
        pairs[i, 1 - low] = weights_other


def newton(place, *operands):
    whole = pl.BlockSpec(memory_space=pltpu.VMEM)
    row = jax.ShapeDtypeStruct((ROWS, H), f32)
    return pl.pallas_call(
        newton_kernel,
        in_specs=[pl.BlockSpec(memory_space=pltpu.SMEM)] + [whole] * 6,
        out_specs=[whole] * 3,
        out_shape=[row, row, jax.ShapeDtypeStruct((16, 2, ROWS, H), bf16)],
        scratch_shapes=[pltpu.VMEM((H, H), f32)] + [pltpu.VMEM((H, H), bf16)] * 4,
        compiler_params=pltpu.CompilerParams(vmem_limit_bytes=56 * 2**20),
        name="newton",
    )(place, *operands)


def exchange(x, axes):
    return lax.all_to_all(x, axes, 0, 0, tiled=True)


def swap(x, axis):
    return lax.ppermute(x, axis, [(0, 1), (1, 0)])


def repeat(x, n):
    return jnp.broadcast_to(x[None], (n,) + x.shape)


def pick(x, axis, index):
    return lax.dynamic_index_in_dim(x, index, axis, keepdims=False)


def late_kernel(given, grads, out, sems):
    copies = []
    for xl in range(2):
        for c in range(2):
            copy = pltpu.make_async_copy(
                grads.at[:, xl, c, :, pl.ds(WIDE, WIDE)], out.at[:, c, xl], sems.at[2 * xl + c]
            )
            copy.start()
            copies.append(copy)
    for copy in copies:
        copy.wait()


def late_columns(given, grads):
    return pl.pallas_call(
        late_kernel,
        in_specs=[pl.BlockSpec(memory_space=pl.ANY), pl.BlockSpec(memory_space=pltpu.HBM)],
        out_specs=pl.BlockSpec(memory_space=pltpu.VMEM),
        out_shape=jax.ShapeDtypeStruct((16, 2, 2, ROWS, WIDE), bf16),
        scratch_shapes=[pltpu.SemaphoreType.DMA((4,))],
        compiler_params=pltpu.CompilerParams(vmem_limit_bytes=16 * 2**20),
        name="late_columns",
    )(given, grads)


def summed_parts(place, grads, master):
    low, core = place[0], place[1]
    grads = grads.reshape(16, 2, 2, ROWS, H)

    def left(c):
        block = lax.dynamic_slice(grads, (0, 0, c, 0, 0), (16, 2, 1, ROWS, WIDE))
        return block.reshape(16, 2, ROWS, WIDE)

    given = left(1 - core)
    swapped = swap(given, "c")
    late = late_columns(given, grads).reshape(32, 2 * ROWS, WIDE)
    late = exchange(late, ("z", "y", "c"))
    early = left(core).astype(f32) + swapped.astype(f32)
    early = pick(early, 1, low) + swap(pick(early, 1, 1 - low), "xl")
    late = late.astype(f32).sum(0).reshape(2, ROWS, WIDE)
    late_other = swap(pick(late, 0, 1 - low), "xl")
    late_other, master = lax.optimization_barrier((late_other, master))
    master_other = swap(master, "xl")
    early, master_other = lax.optimization_barrier((exchange(early, ("z", "y")), master_other))
    return early, pick(late, 0, low), late_other, master_other


def summed_gram(kept, given, ready):
    part = kept + swap(given, "c")
    piece = exchange(part.reshape(64, -1, 128), CHIPS).sum(0)
    piece, ready = lax.optimization_barrier((piece, ready))
    mine = exchange(repeat(piece, 64), CHIPS).reshape(PACKED // 2, 128)
    return mine, swap(mine, "c"), ready


def place_kernel(which, place, piece, *refs):
    out, sem = refs[-2:]
    copy = pltpu.make_async_copy(piece, out.at[:, place[which]], sem)
    copy.start()
    copy.wait()


def placed(place, piece, which, held=None):
    rest = [] if held is None else [held]
    return pl.pallas_call(
        functools.partial(place_kernel, which),
        in_specs=[pl.BlockSpec(memory_space=pltpu.SMEM)]
        + [pl.BlockSpec(memory_space=pltpu.VMEM)]
        + [pl.BlockSpec(memory_space=pltpu.HBM)] * len(rest),
        out_specs=pl.BlockSpec(memory_space=pltpu.HBM),
        out_shape=jax.ShapeDtypeStruct((32, 2, ROWS, H), bf16),
        input_output_aliases={2: 0} if rest else {},
        scratch_shapes=[pltpu.SemaphoreType.DMA],
        compiler_params=pltpu.CompilerParams(vmem_limit_bytes=16 * 2**20),
        name="placed",
    )(place, piece, *rest)


def gathered(place, pairs):
    mine = exchange(pairs, ("z", "y")).reshape(32, ROWS, H)
    other = swap(mine, "c")
    whole = placed(place, other, 2, placed(place, mine, 1))
    return whole.reshape(1, N_DP * ROWS, H)


def shards(grad_parts, master, momentum):
    core, low = lax.axis_index("c"), lax.axis_index("xl")
    place = jnp.stack([low, core, 1 - core]).astype(jnp.int32)
    master = master.reshape(ROWS, H)
    early, late, late_other, master_other = summed_parts(place, grad_parts, master)
    new_momentum, direction, kept, given = direction_and_gram(
        place, early, late, late_other, momentum.reshape(ROWS, H)
    )
    direction_other = swap(direction, "xl")
    mine, other, direction_other = summed_gram(kept, given, direction_other)
    update, new_master, pairs = newton(
        place, mine, other, direction, direction_other, master, master_other
    )
    return (
        gathered(place, pairs),
        new_momentum.reshape(momentum.shape),
        new_master.reshape(momentum.shape),
        update.reshape(momentum.shape),
    )


def solution(mesh):
    fine = Mesh(mesh.devices.reshape(4, 4, 2, 2, 2), ("z", "y", "xl", "c", "xh"))
    rows = P(None, "xh", DP, None)
    return jax.shard_map(
        shards,
        mesh=fine,
        in_specs=(P(DP, None, "xh", None), rows, rows),
        out_specs=(P(None, "xh", None), rows, rows, rows),
        check_vma=False,
    )
```

```python
import functools

import jax
import jax.numpy as jnp
import numpy as np
from jax import lax
from jax.experimental import pallas as pl
from jax.experimental.pallas import tpu as pltpu
from jax.sharding import Mesh, PartitionSpec as P

D = 7168
H = 1024
ITERS = 3
N_DP = 64
ROWS = 56
BLOCK = 256
UPPER = [(i, j) for i in range(H // BLOCK) for j in range(i, H // BLOCK)]
PACKED = len(UPPER) * BLOCK * BLOCK // 128

beta_rate = 0.95
learn_rate = 0.02
decay_rate = 0.1
small_eps = 1e-07
coef_first = 3.4445
coef_second = -4.775
coef_third = 2.0315

f32 = jnp.float32
bf16 = jnp.bfloat16
CHIPS = ("z", "y", "xl", "xh")
DP = ("z", "y", "xl", "c")


def split(x):
    hi = x.astype(bf16)
    return hi, (x - hi.astype(f32)).astype(bf16)


def dot(a, b):
    return jnp.dot(a, b, preferred_element_type=f32)


WIDE = H // 2
QUARTER = PACKED // 4


def place_of(slab):
    return slab // 10, slab % 10 // 5, slab % 5 * BLOCK


def gram_kernel(
    place_ref, early, early_other, late, late_given, momentum, momentum_other,
    new_momentum, direction, kept, given,
):
    low = place_ref[0]

    def moved(left, right, old):
        grad = jnp.concatenate([left[...], right], axis=1)
        new = beta_rate * old[...] + grad
        return new, grad + beta_rate * new

    new, direct = moved(early, late[low] + late_given[low], momentum)
    _, direct_other = moved(early_other, late[1 - low] + late_given[1 - low], momentum_other)
    new_momentum[...] = new
    direct = jnp.concatenate([direct, direct_other], axis=0)
    direction[...] = direct
    hi, lo = split(direct)
    tall = jnp.concatenate([hi, lo, hi, lo], axis=0).T
    deep = jnp.concatenate([hi, hi, lo, lo], axis=0)
    for b, (i, j) in enumerate(UPPER):

        @pl.when(low == b // 5)
        def _():
            tile = dot(tall[i * BLOCK : (i + 1) * BLOCK], deep[:, j * BLOCK : (j + 1) * BLOCK])
            for side in range(2):
                _, core, at = place_of(2 * b + side)
                value = tile[:, side * 128 : (side + 1) * 128]

                @pl.when(place_ref[1] == core)
                def _():
                    kept[pl.ds(at, BLOCK), :] = value

                @pl.when(place_ref[1] != core)
                def _():
                    given[pl.ds(at, BLOCK), :] = value


def direction_and_gram(place, *operands):
    whole = pl.BlockSpec(memory_space=pltpu.VMEM)
    row = jax.ShapeDtypeStruct((ROWS, H), f32)
    rows = jax.ShapeDtypeStruct((2 * ROWS, H), f32)
    quarter = jax.ShapeDtypeStruct((QUARTER, 128), f32)
    return pl.pallas_call(
        gram_kernel,
        in_specs=[pl.BlockSpec(memory_space=pltpu.SMEM)] + [whole] * 6,
        out_specs=[whole] * 4,
        out_shape=[row, rows, quarter, quarter],
        compiler_params=pltpu.CompilerParams(vmem_limit_bytes=24 * 2**20),
        name="direction_and_gram",
    )(place, *operands)


def newton_kernel(
    place_ref, mine, other, direction, master, master_other,
    update, new_master, pairs, gram, g_hi, g_lo, p_hi, p_lo,
):
    n = H // BLOCK
    spans = [slice(i * BLOCK, (i + 1) * BLOCK) for i in range(n)]
    on = lax.broadcasted_iota(jnp.int32, (BLOCK, BLOCK), 0) == lax.broadcasted_iota(
        jnp.int32, (BLOCK, BLOCK), 1
    )
    first_core = place_ref[1] == 0

    def loaded(place):
        low, core, at = place_of(place // BLOCK)
        at += low * QUARTER
        a, b = mine[pl.ds(at, BLOCK), :], other[pl.ds(at, BLOCK), :]
        return jnp.where(first_core, a, b) if core == 0 else jnp.where(first_core, b, a)

    def put(value, i, j, hi_ref, lo_ref):
        hi, lo = split(value)
        hi_ref[spans[i], spans[j]] = hi
        lo_ref[spans[i], spans[j]] = lo
        if j > i:
            hi_ref[spans[j], spans[i]] = hi.T
            lo_ref[spans[j], spans[i]] = lo.T

    def full(a_hi, a_lo, b_hi, b_lo, i):
        cols = slice(i * BLOCK, H)
        b = b_hi[:, cols]
        return (
            dot(a_hi[spans[i], :], b)
            + dot(a_lo[spans[i], :], b)
            + dot(a_hi[spans[i], :], b_lo[:, cols])
        )

    def thin(x, b_hi, b_lo):
        hi, lo = split(x)
        both = dot(jnp.concatenate([hi, lo], axis=0), b_hi[...])
        return both[: 2 * ROWS] + both[2 * ROWS :] + dot(hi, b_lo[...])

    def poly():
        for i in range(n):
            square = full(g_hi, g_lo, g_hi, g_lo, i)
            for j in range(i, n):
                value = coef_second * gram[spans[i], spans[j]]
                value += coef_third * square[:, (j - i) * BLOCK : (j - i + 1) * BLOCK]
                if i == j:
                    value += jnp.where(on, coef_first, 0.0)
                put(value, i, j, p_hi, p_lo)

    def times_poly():
        for i in range(n):
            gram[spans[i], i * BLOCK :] = full(g_hi, g_lo, p_hi, p_lo, i)
        for i in range(n):
            for j in range(i, n):
                put(gram[spans[i], spans[j]], i, j, g_hi, g_lo)

    place = 0
    trace = jnp.zeros((), f32)
    for i in range(n):
        for j in range(i, n):
            tile = jnp.concatenate([loaded(place), loaded(place + BLOCK)], axis=1)
            place += 2 * BLOCK
            gram[spans[i], spans[j]] = tile
            if i == j:
                trace += jnp.sum(jnp.where(on, tile, 0.0))
    inverse = 1.0 / (jnp.sqrt(jnp.full((1, 1), trace, f32)) + small_eps)
    for i in range(n):
        for j in range(i, n):
            value = gram[spans[i], spans[j]] * inverse * inverse
            gram[spans[i], spans[j]] = value
            put(value, i, j, g_hi, g_lo)

    scaled = direction[...] * inverse
    poly()
    scaled = thin(scaled, p_hi, p_lo)
    times_poly()
    times_poly()
    poly()
    scaled = thin(scaled, p_hi, p_lo)

    def last_gram(x):
        return thin(thin(thin(x, p_hi, p_lo), p_hi, p_lo), g_hi, g_lo)

    once = last_gram(scaled)
    twice = last_gram(once)
    scaled = coef_first * scaled + coef_second * once + coef_third * twice
    result = (0.2 * max(D, H) ** 0.5) * scaled
    update[...] = result[:ROWS]

    def stepped(old, change):
        return old * (1.0 - learn_rate * decay_rate) - learn_rate * change

    moved = stepped(master[...], result[:ROWS])
    new_master[...] = moved
    weights = moved.astype(bf16)
    weights_other = stepped(master_other[...], result[ROWS:]).astype(bf16)
    low = place_ref[0]
    for i in range(16):
        pairs[i, low] = weights
        pairs[i, 1 - low] = weights_other


def newton(place, *operands):
    whole = pl.BlockSpec(memory_space=pltpu.VMEM)
    row = jax.ShapeDtypeStruct((ROWS, H), f32)
    return pl.pallas_call(
        newton_kernel,
        in_specs=[pl.BlockSpec(memory_space=pltpu.SMEM)] + [whole] * 5,
        out_specs=[whole] * 3,
        out_shape=[row, row, jax.ShapeDtypeStruct((16, 2, ROWS, H), bf16)],
        scratch_shapes=[pltpu.VMEM((H, H), f32)] + [pltpu.VMEM((H, H), bf16)] * 4,
        compiler_params=pltpu.CompilerParams(vmem_limit_bytes=56 * 2**20),
        name="newton",
    )(place, *operands)


def exchange(x, axes):
    return lax.all_to_all(x, axes, 0, 0, tiled=True)


def swap(x, axis):
    return lax.ppermute(x, axis, [(0, 1), (1, 0)])


def repeat(x, n):
    return jnp.broadcast_to(x[None], (n,) + x.shape)


def pick(x, axis, index):
    return lax.dynamic_index_in_dim(x, index, axis, keepdims=False)


def late_kernel(given, grads, out, sems):
    copies = []
    for xl in range(2):
        for c in range(2):
            copy = pltpu.make_async_copy(
                grads.at[:, xl, c, :, pl.ds(WIDE, WIDE)], out.at[:, c, xl], sems.at[2 * xl + c]
            )
            copy.start()
            copies.append(copy)
    for copy in copies:
        copy.wait()


def late_columns(given, grads):
    return pl.pallas_call(
        late_kernel,
        in_specs=[pl.BlockSpec(memory_space=pl.ANY), pl.BlockSpec(memory_space=pltpu.HBM)],
        out_specs=pl.BlockSpec(memory_space=pltpu.VMEM),
        out_shape=jax.ShapeDtypeStruct((16, 2, 2, ROWS, WIDE), bf16),
        scratch_shapes=[pltpu.SemaphoreType.DMA((4,))],
        compiler_params=pltpu.CompilerParams(vmem_limit_bytes=16 * 2**20),
        name="late_columns",
    )(given, grads)


def summed_parts(place, grads, state):
    low, core = place[0], place[1]
    grads = grads.reshape(16, 2, 2, ROWS, H)

    def left(c):
        block = lax.dynamic_slice(grads, (0, 0, c, 0, 0), (16, 2, 1, ROWS, WIDE))
        return block.reshape(16, 2, ROWS, WIDE)

    given = left(1 - core)
    swapped = swap(given, "c")
    late = late_columns(given, grads).reshape(32, 2 * ROWS, WIDE)
    late = exchange(late, ("z", "y", "c"))
    early = left(core).astype(f32) + swapped.astype(f32)
    early = pick(early, 1, low) + swap(pick(early, 1, 1 - low), "xl")
    late = late.astype(f32).sum(0).reshape(2, ROWS, WIDE)
    late_given, state = lax.optimization_barrier((swap(late, "xl"), state))
    state_other = swap(state, "xl")
    early, state_other = lax.optimization_barrier((exchange(early, ("z", "y")), state_other))
    early = early.sum(0)
    return (early, swap(early, "xl"), late, late_given), state_other


def summed_gram(kept, given):
    part = kept + swap(given, "c")
    piece = exchange(part.reshape(32, -1, 128), ("z", "y", "xh")).sum(0)
    mine = exchange(repeat(piece, 64), ("xl", "z", "y", "xh")).reshape(2 * QUARTER, 128)
    return mine, swap(mine, "c")


def place_kernel(which, place, piece, *refs):
    out, sem = refs[-2:]
    copy = pltpu.make_async_copy(piece, out.at[:, place[which]], sem)
    copy.start()
    copy.wait()


def placed(place, piece, which, held=None):
    rest = [] if held is None else [held]
    return pl.pallas_call(
        functools.partial(place_kernel, which),
        in_specs=[pl.BlockSpec(memory_space=pltpu.SMEM)]
        + [pl.BlockSpec(memory_space=pltpu.VMEM)]
        + [pl.BlockSpec(memory_space=pltpu.HBM)] * len(rest),
        out_specs=pl.BlockSpec(memory_space=pltpu.HBM),
        out_shape=jax.ShapeDtypeStruct((32, 2, ROWS, H), bf16),
        input_output_aliases={2: 0} if rest else {},
        scratch_shapes=[pltpu.SemaphoreType.DMA],
        compiler_params=pltpu.CompilerParams(vmem_limit_bytes=16 * 2**20),
        name="placed",
    )(place, piece, *rest)


def gathered(place, pairs):
    mine = exchange(pairs, ("z", "y")).reshape(32, ROWS, H)
    other = swap(mine, "c")
    whole = placed(place, other, 2, placed(place, mine, 1))
    return whole.reshape(1, N_DP * ROWS, H)


def shards(grad_parts, master, momentum):
    core, low = lax.axis_index("c"), lax.axis_index("xl")
    place = jnp.stack([low, core, 1 - core]).astype(jnp.int32)
    shape = master.shape
    master = master.reshape(ROWS, H)
    momentum = momentum.reshape(ROWS, H)
    sums, state_other = summed_parts(place, grad_parts, jnp.concatenate([momentum, master]))
    new_momentum, direction, kept, given = direction_and_gram(
        place, *sums, momentum, state_other[:ROWS]
    )
    mine, other = summed_gram(kept, given)
    update, new_master, pairs = newton(
        place, mine, other, direction, master, state_other[ROWS:]
    )
    return (
        gathered(place, pairs),
        new_momentum.reshape(shape),
        new_master.reshape(shape),
        update.reshape(shape),
    )


def solution(mesh):
    fine = Mesh(mesh.devices.reshape(4, 4, 2, 2, 2), ("z", "y", "xl", "c", "xh"))
    rows = P(None, "xh", DP, None)
    return jax.shard_map(
        shards,
        mesh=fine,
        in_specs=(P(DP, None, "xh", None), rows, rows),
        out_specs=(P(None, "xh", None), rows, rows, rows),
        check_vma=False,
    )
```

```python
import functools

import jax
import jax.numpy as jnp
import numpy as np
from jax import lax
from jax.experimental import pallas as pl
from jax.experimental.pallas import tpu as pltpu
from jax.sharding import Mesh, PartitionSpec as P

D = 7168
H = 1024
ITERS = 3
N_DP = 64
ROWS = 56
BLOCK = 256
UPPER = [(i, j) for i in range(H // BLOCK) for j in range(i, H // BLOCK)]
PACKED = len(UPPER) * BLOCK * BLOCK // 128

beta_rate = 0.95
learn_rate = 0.02
decay_rate = 0.1
small_eps = 1e-07
coef_first = 3.4445
coef_second = -4.775
coef_third = 2.0315

f32 = jnp.float32
bf16 = jnp.bfloat16
CHIPS = ("z", "y", "xl", "xh")
DP = ("z", "y", "xl", "c")


def split(x):
    hi = x.astype(bf16)
    return hi, (x - hi.astype(f32)).astype(bf16)


def dot(a, b):
    return jnp.dot(a, b, preferred_element_type=f32)


WIDE = H // 2
QUARTER = PACKED // 4


def place_of(slab):
    return slab // 10, slab % 10 // 5, slab % 5 * BLOCK


def gram_kernel(
    place_ref, early, early_other, late, late_given, momentum, momentum_other,
    new_momentum, direction, kept, given,
):
    low = place_ref[0]

    def moved(left, right, old):
        grad = jnp.concatenate([left[...], right], axis=1)
        new = beta_rate * old[...] + grad
        return new, grad + beta_rate * new

    new, direct = moved(early, late[low] + late_given[low], momentum)
    _, direct_other = moved(early_other, late[1 - low] + late_given[1 - low], momentum_other)
    new_momentum[...] = new
    direct = jnp.concatenate([direct, direct_other], axis=0)
    direction[...] = direct
    hi, lo = split(direct)
    tall = jnp.concatenate([hi, lo, hi, lo], axis=0).T
    deep = jnp.concatenate([hi, hi, lo, lo], axis=0)
    for b, (i, j) in enumerate(UPPER):

        @pl.when(low == b // 5)
        def _():
            tile = dot(tall[i * BLOCK : (i + 1) * BLOCK], deep[:, j * BLOCK : (j + 1) * BLOCK])
            for side in range(2):
                _, core, at = place_of(2 * b + side)
                value = tile[:, side * 128 : (side + 1) * 128]

                @pl.when(place_ref[1] == core)
                def _():
                    kept[pl.ds(at, BLOCK), :] = value

                @pl.when(place_ref[1] != core)
                def _():
                    given[pl.ds(at, BLOCK), :] = value


def direction_and_gram(place, *operands):
    whole = pl.BlockSpec(memory_space=pltpu.VMEM)
    row = jax.ShapeDtypeStruct((ROWS, H), f32)
    rows = jax.ShapeDtypeStruct((2 * ROWS, H), f32)
    quarter = jax.ShapeDtypeStruct((QUARTER, 128), f32)
    return pl.pallas_call(
        gram_kernel,
        in_specs=[pl.BlockSpec(memory_space=pltpu.SMEM)] + [whole] * 6,
        out_specs=[whole] * 4,
        out_shape=[row, rows, quarter, quarter],
        compiler_params=pltpu.CompilerParams(vmem_limit_bytes=24 * 2**20),
        name="direction_and_gram",
    )(place, *operands)


def newton_kernel(
    place_ref, mine, other, direction, master, master_other,
    update, new_master, pairs, gram, g_hi, g_lo, p_hi, p_lo,
):
    n = H // BLOCK
    spans = [slice(i * BLOCK, (i + 1) * BLOCK) for i in range(n)]
    on = lax.broadcasted_iota(jnp.int32, (BLOCK, BLOCK), 0) == lax.broadcasted_iota(
        jnp.int32, (BLOCK, BLOCK), 1
    )
    first_core = place_ref[1] == 0

    def loaded(place):
        low, core, at = place_of(place // BLOCK)
        at += low * QUARTER
        a, b = mine[pl.ds(at, BLOCK), :], other[pl.ds(at, BLOCK), :]
        return jnp.where(first_core, a, b) if core == 0 else jnp.where(first_core, b, a)

    def put(value, i, j, hi_ref, lo_ref):
        hi, lo = split(value)
        hi_ref[spans[i], spans[j]] = hi
        lo_ref[spans[i], spans[j]] = lo
        if j > i:
            hi_ref[spans[j], spans[i]] = hi.T
            lo_ref[spans[j], spans[i]] = lo.T

    def full(a_hi, a_lo, b_hi, b_lo, i):
        cols = slice(i * BLOCK, H)
        b = b_hi[:, cols]
        return (
            dot(a_hi[spans[i], :], b)
            + dot(a_lo[spans[i], :], b)
            + dot(a_hi[spans[i], :], b_lo[:, cols])
        )

    def thin(x, b_hi, b_lo):
        hi, lo = split(x)
        both = dot(jnp.concatenate([hi, lo], axis=0), b_hi[...])
        return both[: 2 * ROWS] + both[2 * ROWS :] + dot(hi, b_lo[...])

    def poly():
        for i in range(n):
            square = full(g_hi, g_lo, g_hi, g_lo, i)
            for j in range(i, n):
                value = coef_second * gram[spans[i], spans[j]]
                value += coef_third * square[:, (j - i) * BLOCK : (j - i + 1) * BLOCK]
                if i == j:
                    value += jnp.where(on, coef_first, 0.0)
                put(value, i, j, p_hi, p_lo)

    def times_poly():
        for i in range(n):
            gram[spans[i], i * BLOCK :] = full(g_hi, g_lo, p_hi, p_lo, i)
        for i in range(n):
            for j in range(i, n):
                put(gram[spans[i], spans[j]], i, j, g_hi, g_lo)

    place = 0
    trace = jnp.zeros((), f32)
    for i in range(n):
        for j in range(i, n):
            tile = jnp.concatenate([loaded(place), loaded(place + BLOCK)], axis=1)
            place += 2 * BLOCK
            gram[spans[i], spans[j]] = tile
            if i == j:
                trace += jnp.sum(jnp.where(on, tile, 0.0))
    inverse = 1.0 / (jnp.sqrt(jnp.full((1, 1), trace, f32)) + small_eps)
    for i in range(n):
        for j in range(i, n):
            value = gram[spans[i], spans[j]] * inverse * inverse
            gram[spans[i], spans[j]] = value
            put(value, i, j, g_hi, g_lo)

    scaled = direction[...] * inverse
    poly()
    scaled = thin(scaled, p_hi, p_lo)
    times_poly()
    times_poly()
    poly()
    scaled = thin(scaled, p_hi, p_lo)

    def last_gram(x):
        return thin(thin(thin(x, p_hi, p_lo), p_hi, p_lo), g_hi, g_lo)

    once = last_gram(scaled)
    twice = last_gram(once)
    scaled = coef_first * scaled + coef_second * once + coef_third * twice
    result = (0.2 * max(D, H) ** 0.5) * scaled
    update[...] = result[:ROWS]

    def stepped(old, change):
        return old * (1.0 - learn_rate * decay_rate) - learn_rate * change

    moved = stepped(master[...], result[:ROWS])
    new_master[...] = moved
    weights = moved.astype(bf16)
    weights_other = stepped(master_other[...], result[ROWS:]).astype(bf16)
    low = place_ref[0]
    for i in range(16):
        pairs[i, low] = weights
        pairs[i, 1 - low] = weights_other


def newton(place, *operands):
    whole = pl.BlockSpec(memory_space=pltpu.VMEM)
    row = jax.ShapeDtypeStruct((ROWS, H), f32)
    return pl.pallas_call(
        newton_kernel,
        in_specs=[pl.BlockSpec(memory_space=pltpu.SMEM)] + [whole] * 5,
        out_specs=[whole] * 3,
        out_shape=[row, row, jax.ShapeDtypeStruct((16, 2, ROWS, H), bf16)],
        scratch_shapes=[pltpu.VMEM((H, H), f32)] + [pltpu.VMEM((H, H), bf16)] * 4,
        compiler_params=pltpu.CompilerParams(vmem_limit_bytes=56 * 2**20),
        name="newton",
    )(place, *operands)


def exchange(x, axes):
    return lax.all_to_all(x, axes, 0, 0, tiled=True)


def swap(x, axis):
    return lax.ppermute(x, axis, [(0, 1), (1, 0)])


def repeat(x, n):
    return jnp.broadcast_to(x[None], (n,) + x.shape)


def pick(x, axis, index):
    return lax.dynamic_index_in_dim(x, index, axis, keepdims=False)


def late_kernel(given, grads, out, held, sems, out_sems):
    parts = [(xl, c) for xl in range(2) for c in range(2)]
    into = [
        pltpu.make_async_copy(
            grads.at[:, xl, c, :, pl.ds(WIDE, WIDE)], held.at[2 * xl + c], sems.at[2 * xl + c]
        )
        for xl, c in parts
    ]
    away = [
        pltpu.make_async_copy(held.at[2 * xl + c], out.at[:, c, xl], out_sems.at[2 * xl + c])
        for xl, c in parts
    ]
    for copy in into:
        copy.start()
    for copy, back in zip(into, away):
        copy.wait()
        back.start()
    for back in away:
        back.wait()


def late_columns(given, grads):
    return pl.pallas_call(
        late_kernel,
        in_specs=[pl.BlockSpec(memory_space=pl.ANY)] * 2,
        out_specs=pl.BlockSpec(memory_space=pltpu.HBM),
        out_shape=jax.ShapeDtypeStruct((16, 2, 2, ROWS, WIDE), bf16),
        scratch_shapes=[
            pltpu.VMEM((4, 16, ROWS, WIDE), bf16),
            pltpu.SemaphoreType.DMA((4,)),
            pltpu.SemaphoreType.DMA((4,)),
        ],
        compiler_params=pltpu.CompilerParams(vmem_limit_bytes=52 * 2**20),
        name="late_columns",
    )(given, grads)


def early_kernel(place, grads, swapped, kept, given, held, sems):
    low, core = place[0], place[1]
    copies = [
        pltpu.make_async_copy(
            grads.at[:, xl, core, :, pl.ds(0, WIDE)], held.at[xl], sems.at[xl]
        )
        for xl in range(2)
    ]
    for copy in copies:
        copy.start()
    for copy in copies:
        copy.wait()
    for k in range(16):
        given[k] = held[1 - low, k].astype(f32) + swapped[k, 1 - low].astype(f32)
    for k in range(16):
        kept[k] = held[low, k].astype(f32) + swapped[k, low].astype(f32)


def early_sums(place, grads, swapped):
    whole = pl.BlockSpec(memory_space=pltpu.VMEM)
    half = jax.ShapeDtypeStruct((16, ROWS, WIDE), f32)
    return pl.pallas_call(
        early_kernel,
        in_specs=[
            pl.BlockSpec(memory_space=pltpu.SMEM),
            pl.BlockSpec(memory_space=pl.ANY),
            whole,
        ],
        out_specs=[whole, whole],
        out_shape=[half, half],
        scratch_shapes=[pltpu.VMEM((2, 16, ROWS, WIDE), bf16), pltpu.SemaphoreType.DMA((2,))],
        compiler_params=pltpu.CompilerParams(vmem_limit_bytes=48 * 2**20),
        name="early_sums",
    )(place, grads, swapped)


def summed_parts(place, grads, state):
    core = place[1]
    grads = grads.reshape(16, 2, 2, ROWS, H)

    def left(c):
        block = lax.dynamic_slice(grads, (0, 0, c, 0, 0), (16, 2, 1, ROWS, WIDE))
        return block.reshape(16, 2, ROWS, WIDE)

    given = left(1 - core)
    swapped = swap(given, "c")
    late = late_columns(given, grads).reshape(32, 2 * ROWS, WIDE)
    late = exchange(late, ("z", "y", "c"))
    kept, given = early_sums(place, grads, swapped)
    early = kept + swap(given, "xl")
    late = late.astype(f32).sum(0).reshape(2, ROWS, WIDE)
    late_given, state = lax.optimization_barrier((swap(late, "xl"), state))
    state_other = swap(state, "xl")
    early, state_other = lax.optimization_barrier((exchange(early, ("z", "y")), state_other))
    early = early.sum(0)
    return (early, swap(early, "xl"), late, late_given), state_other


def summed_gram(kept, given):
    part = kept + swap(given, "c")
    piece = exchange(part.reshape(32, -1, 128), ("z", "y", "xh")).sum(0)
    mine = exchange(repeat(piece, 64), ("xl", "z", "y", "xh")).reshape(2 * QUARTER, 128)
    return mine, swap(mine, "c")


def place_kernel(which, place, piece, *refs):
    out, sem = refs[-2:]
    copy = pltpu.make_async_copy(piece, out.at[:, place[which]], sem)
    copy.start()
    copy.wait()


def placed(place, piece, which, held=None):
    rest = [] if held is None else [held]
    return pl.pallas_call(
        functools.partial(place_kernel, which),
        in_specs=[pl.BlockSpec(memory_space=pltpu.SMEM)]
        + [pl.BlockSpec(memory_space=pltpu.VMEM)]
        + [pl.BlockSpec(memory_space=pltpu.HBM)] * len(rest),
        out_specs=pl.BlockSpec(memory_space=pltpu.HBM),
        out_shape=jax.ShapeDtypeStruct((32, 2, ROWS, H), bf16),
        input_output_aliases={2: 0} if rest else {},
        scratch_shapes=[pltpu.SemaphoreType.DMA],
        compiler_params=pltpu.CompilerParams(vmem_limit_bytes=16 * 2**20),
        name="placed",
    )(place, piece, *rest)


def gathered(place, pairs):
    mine = exchange(pairs, ("z", "y")).reshape(32, ROWS, H)
    other = swap(mine, "c")
    whole = placed(place, other, 2, placed(place, mine, 1))
    return whole.reshape(1, N_DP * ROWS, H)


def shards(grad_parts, master, momentum):
    core, low = lax.axis_index("c"), lax.axis_index("xl")
    place = jnp.stack([low, core, 1 - core]).astype(jnp.int32)
    shape = master.shape
    master = master.reshape(ROWS, H)
    momentum = momentum.reshape(ROWS, H)
    sums, state_other = summed_parts(place, grad_parts, jnp.concatenate([momentum, master]))
    new_momentum, direction, kept, given = direction_and_gram(
        place, *sums, momentum, state_other[:ROWS]
    )
    mine, other = summed_gram(kept, given)
    update, new_master, pairs = newton(
        place, mine, other, direction, master, state_other[ROWS:]
    )
    return (
        gathered(place, pairs),
        new_momentum.reshape(shape),
        new_master.reshape(shape),
        update.reshape(shape),
    )


def solution(mesh):
    fine = Mesh(mesh.devices.reshape(4, 4, 2, 2, 2), ("z", "y", "xl", "c", "xh"))
    rows = P(None, "xh", DP, None)
    return jax.shard_map(
        shards,
        mesh=fine,
        in_specs=(P(DP, None, "xh", None), rows, rows),
        out_specs=(P(None, "xh", None), rows, rows, rows),
        check_vma=False,
    )
```

```python
import functools

import jax
import jax.numpy as jnp
import numpy as np
from jax import lax
from jax.experimental import pallas as pl
from jax.experimental.pallas import tpu as pltpu
from jax.sharding import Mesh, PartitionSpec as P

D = 7168
H = 1024
ITERS = 3
N_DP = 64
ROWS = 56
BLOCK = 256
UPPER = [(i, j) for i in range(H // BLOCK) for j in range(i, H // BLOCK)]
PACKED = len(UPPER) * BLOCK * BLOCK // 128

beta_rate = 0.95
learn_rate = 0.02
decay_rate = 0.1
small_eps = 1e-07
coef_first = 3.4445
coef_second = -4.775
coef_third = 2.0315

f32 = jnp.float32
bf16 = jnp.bfloat16
CHIPS = ("z", "y", "xl", "xh")
DP = ("z", "y", "xl", "c")


def split(x):
    hi = x.astype(bf16)
    return hi, (x - hi.astype(f32)).astype(bf16)


def dot(a, b):
    return jnp.dot(a, b, preferred_element_type=f32)


WIDE = H // 2
QUARTER = PACKED // 4


def place_of(slab):
    return slab // 10, slab % 10 // 5, slab % 5 * BLOCK


def gram_kernel(
    place_ref, early, early_other, late, late_given, momentum, momentum_other,
    new_momentum, direction, kept, given,
):
    low = place_ref[0]

    def moved(left, right, old):
        grad = jnp.concatenate([left[...], right], axis=1)
        new = beta_rate * old[...] + grad
        return new, grad + beta_rate * new

    new, direct = moved(early, late[low] + late_given[low], momentum)
    _, direct_other = moved(early_other, late[1 - low] + late_given[1 - low], momentum_other)
    new_momentum[...] = new
    direct = jnp.concatenate([direct, direct_other], axis=0)
    direction[...] = direct
    hi, lo = split(direct)
    tall = jnp.concatenate([hi, lo, hi, lo], axis=0).T
    deep = jnp.concatenate([hi, hi, lo, lo], axis=0)
    for b, (i, j) in enumerate(UPPER):

        @pl.when(low == b // 5)
        def _():
            tile = dot(tall[i * BLOCK : (i + 1) * BLOCK], deep[:, j * BLOCK : (j + 1) * BLOCK])
            for side in range(2):
                _, core, at = place_of(2 * b + side)
                value = tile[:, side * 128 : (side + 1) * 128]

                @pl.when(place_ref[1] == core)
                def _():
                    kept[pl.ds(at, BLOCK), :] = value

                @pl.when(place_ref[1] != core)
                def _():
                    given[pl.ds(at, BLOCK), :] = value


def direction_and_gram(place, *operands):
    whole = pl.BlockSpec(memory_space=pltpu.VMEM)
    row = jax.ShapeDtypeStruct((ROWS, H), f32)
    rows = jax.ShapeDtypeStruct((2 * ROWS, H), f32)
    quarter = jax.ShapeDtypeStruct((QUARTER, 128), f32)
    return pl.pallas_call(
        gram_kernel,
        in_specs=[pl.BlockSpec(memory_space=pltpu.SMEM)] + [whole] * 6,
        out_specs=[whole] * 4,
        out_shape=[row, rows, quarter, quarter],
        compiler_params=pltpu.CompilerParams(vmem_limit_bytes=24 * 2**20),
        name="direction_and_gram",
    )(place, *operands)


def newton_kernel(
    place_ref, mine, other, direction, master, master_other,
    update, new_master, left, right, gram, g_hi, g_lo, p_hi, p_lo,
):
    n = H // BLOCK
    spans = [slice(i * BLOCK, (i + 1) * BLOCK) for i in range(n)]
    on = lax.broadcasted_iota(jnp.int32, (BLOCK, BLOCK), 0) == lax.broadcasted_iota(
        jnp.int32, (BLOCK, BLOCK), 1
    )
    first_core = place_ref[1] == 0

    def loaded(place):
        low, core, at = place_of(place // BLOCK)
        at += low * QUARTER
        a, b = mine[pl.ds(at, BLOCK), :], other[pl.ds(at, BLOCK), :]
        return jnp.where(first_core, a, b) if core == 0 else jnp.where(first_core, b, a)

    def put(value, i, j, hi_ref, lo_ref):
        hi, lo = split(value)
        hi_ref[spans[i], spans[j]] = hi
        lo_ref[spans[i], spans[j]] = lo
        if j > i:
            hi_ref[spans[j], spans[i]] = hi.T
            lo_ref[spans[j], spans[i]] = lo.T

    def full(a_hi, a_lo, b_hi, b_lo, i):
        cols = slice(i * BLOCK, H)
        b = b_hi[:, cols]
        return (
            dot(a_hi[spans[i], :], b)
            + dot(a_lo[spans[i], :], b)
            + dot(a_hi[spans[i], :], b_lo[:, cols])
        )

    def thin(x, b_hi, b_lo):
        hi, lo = split(x)
        both = dot(jnp.concatenate([hi, lo], axis=0), b_hi[...])
        return both[: 2 * ROWS] + both[2 * ROWS :] + dot(hi, b_lo[...])

    def poly():
        for i in range(n):
            square = full(g_hi, g_lo, g_hi, g_lo, i)
            for j in range(i, n):
                value = coef_second * gram[spans[i], spans[j]]
                value += coef_third * square[:, (j - i) * BLOCK : (j - i + 1) * BLOCK]
                if i == j:
                    value += jnp.where(on, coef_first, 0.0)
                put(value, i, j, p_hi, p_lo)

    def times_poly():
        for i in range(n):
            gram[spans[i], i * BLOCK :] = full(g_hi, g_lo, p_hi, p_lo, i)
        for i in range(n):
            for j in range(i, n):
                put(gram[spans[i], spans[j]], i, j, g_hi, g_lo)

    place = 0
    trace = jnp.zeros((), f32)
    for i in range(n):
        for j in range(i, n):
            tile = jnp.concatenate([loaded(place), loaded(place + BLOCK)], axis=1)
            place += 2 * BLOCK
            gram[spans[i], spans[j]] = tile
            if i == j:
                trace += jnp.sum(jnp.where(on, tile, 0.0))
    inverse = 1.0 / (jnp.sqrt(jnp.full((1, 1), trace, f32)) + small_eps)
    for i in range(n):
        for j in range(i, n):
            value = gram[spans[i], spans[j]] * inverse * inverse
            gram[spans[i], spans[j]] = value
            put(value, i, j, g_hi, g_lo)

    scaled = direction[...] * inverse
    poly()
    scaled = thin(scaled, p_hi, p_lo)
    times_poly()
    times_poly()
    poly()
    scaled = thin(scaled, p_hi, p_lo)

    def last_gram(x):
        return thin(thin(thin(x, p_hi, p_lo), p_hi, p_lo), g_hi, g_lo)

    once = last_gram(scaled)
    twice = last_gram(once)
    scaled = coef_first * scaled + coef_second * once + coef_third * twice
    result = (0.2 * max(D, H) ** 0.5) * scaled
    update[...] = result[:ROWS]

    def stepped(old, change):
        return old * (1.0 - learn_rate * decay_rate) - learn_rate * change

    moved = stepped(master[...], result[:ROWS])
    new_master[...] = moved
    weights = moved.astype(bf16)
    weights_other = stepped(master_other[...], result[ROWS:]).astype(bf16)
    low = place_ref[0]
    for at, value in ((low, weights), (1 - low, weights_other)):
        for i in range(4):
            left[i, at] = value[:, :WIDE]
        right[at] = value[:, WIDE:]


def newton(place, *operands):
    whole = pl.BlockSpec(memory_space=pltpu.VMEM)
    row = jax.ShapeDtypeStruct((ROWS, H), f32)
    return pl.pallas_call(
        newton_kernel,
        in_specs=[pl.BlockSpec(memory_space=pltpu.SMEM)] + [whole] * 5,
        out_specs=[whole] * 4,
        out_shape=[
            row,
            row,
            jax.ShapeDtypeStruct((4, 2, ROWS, WIDE), bf16),
            jax.ShapeDtypeStruct((2, ROWS, WIDE), bf16),
        ],
        scratch_shapes=[pltpu.VMEM((H, H), f32)] + [pltpu.VMEM((H, H), bf16)] * 4,
        compiler_params=pltpu.CompilerParams(vmem_limit_bytes=56 * 2**20),
        name="newton",
    )(place, *operands)


def exchange(x, axes):
    return lax.all_to_all(x, axes, 0, 0, tiled=True)


def swap(x, axis):
    return lax.ppermute(x, axis, [(0, 1), (1, 0)])


def repeat(x, n):
    return jnp.broadcast_to(x[None], (n,) + x.shape)


def pick(x, axis, index):
    return lax.dynamic_index_in_dim(x, index, axis, keepdims=False)


def late_kernel(given, grads, out, held, sems, out_sems):
    parts = [(xl, c) for xl in range(2) for c in range(2)]
    into = [
        pltpu.make_async_copy(
            grads.at[:, xl, c, :, pl.ds(WIDE, WIDE)], held.at[2 * xl + c], sems.at[2 * xl + c]
        )
        for xl, c in parts
    ]
    away = [
        pltpu.make_async_copy(held.at[2 * xl + c], out.at[:, c, xl], out_sems.at[2 * xl + c])
        for xl, c in parts
    ]
    for copy in into:
        copy.start()
    for copy, back in zip(into, away):
        copy.wait()
        back.start()
    for back in away:
        back.wait()


def late_columns(given, grads):
    return pl.pallas_call(
        late_kernel,
        in_specs=[pl.BlockSpec(memory_space=pl.ANY)] * 2,
        out_specs=pl.BlockSpec(memory_space=pltpu.HBM),
        out_shape=jax.ShapeDtypeStruct((16, 2, 2, ROWS, WIDE), bf16),
        scratch_shapes=[
            pltpu.VMEM((4, 16, ROWS, WIDE), bf16),
            pltpu.SemaphoreType.DMA((4,)),
            pltpu.SemaphoreType.DMA((4,)),
        ],
        compiler_params=pltpu.CompilerParams(vmem_limit_bytes=52 * 2**20),
        name="late_columns",
    )(given, grads)


def early_kernel(place, grads, swapped, kept, given, held, sems):
    low, core = place[0], place[1]
    copies = [
        pltpu.make_async_copy(
            grads.at[:, xl, core, :, pl.ds(0, WIDE)], held.at[xl], sems.at[xl]
        )
        for xl in range(2)
    ]
    for copy in copies:
        copy.start()
    for copy in copies:
        copy.wait()
    for k in range(16):
        given[k] = held[1 - low, k].astype(f32) + swapped[k, 1 - low].astype(f32)
    for k in range(16):
        kept[k] = held[low, k].astype(f32) + swapped[k, low].astype(f32)


def early_sums(place, grads, swapped):
    whole = pl.BlockSpec(memory_space=pltpu.VMEM)
    half = jax.ShapeDtypeStruct((16, ROWS, WIDE), f32)
    return pl.pallas_call(
        early_kernel,
        in_specs=[
            pl.BlockSpec(memory_space=pltpu.SMEM),
            pl.BlockSpec(memory_space=pl.ANY),
            whole,
        ],
        out_specs=[whole, whole],
        out_shape=[half, half],
        scratch_shapes=[pltpu.VMEM((2, 16, ROWS, WIDE), bf16), pltpu.SemaphoreType.DMA((2,))],
        compiler_params=pltpu.CompilerParams(vmem_limit_bytes=48 * 2**20),
        name="early_sums",
    )(place, grads, swapped)


def summed_parts(place, grads, state):
    core = place[1]
    grads = grads.reshape(16, 2, 2, ROWS, H)

    def left(c):
        block = lax.dynamic_slice(grads, (0, 0, c, 0, 0), (16, 2, 1, ROWS, WIDE))
        return block.reshape(16, 2, ROWS, WIDE)

    given = left(1 - core)
    swapped = swap(given, "c")
    late = late_columns(given, grads).reshape(32, 2 * ROWS, WIDE)
    late = exchange(late, ("z", "y", "c"))
    kept, given = early_sums(place, grads, swapped)
    early = kept + swap(given, "xl")
    late = late.astype(f32).sum(0).reshape(2, ROWS, WIDE)
    late_given, state = lax.optimization_barrier((swap(late, "xl"), state))
    state_other = swap(state, "xl")
    early, state_other = lax.optimization_barrier((exchange(early, ("z", "y")), state_other))
    early = early.sum(0)
    return (early, swap(early, "xl"), late, late_given), state_other


def summed_gram(kept, given):
    part = kept + swap(given, "c")
    piece = exchange(part.reshape(32, -1, 128), ("z", "y", "xh")).sum(0)
    mine = exchange(repeat(piece, 64), ("xl", "z", "y", "xh")).reshape(2 * QUARTER, 128)
    return mine, swap(mine, "c")


def place_kernel(which, place, piece, *refs):
    out, sem = refs[-2:]
    copy = pltpu.make_async_copy(piece, out.at[:, place[which]], sem)
    copy.start()
    copy.wait()


def placed(place, piece, which, held=None):
    rest = [] if held is None else [held]
    return pl.pallas_call(
        functools.partial(place_kernel, which),
        in_specs=[pl.BlockSpec(memory_space=pltpu.SMEM)]
        + [pl.BlockSpec(memory_space=pltpu.VMEM)]
        + [pl.BlockSpec(memory_space=pltpu.HBM)] * len(rest),
        out_specs=pl.BlockSpec(memory_space=pltpu.HBM),
        out_shape=jax.ShapeDtypeStruct((32, 2, ROWS, H), bf16),
        input_output_aliases={2: 0} if rest else {},
        scratch_shapes=[pltpu.SemaphoreType.DMA],
        compiler_params=pltpu.CompilerParams(vmem_limit_bytes=16 * 2**20),
        name="placed",
    )(place, piece, *rest)


def terms_along(x, axis):
    return [x] + [lax.ppermute(x, axis, [(i, (i + by) % 4) for i in range(4)]) for by in (1, 2, 3)]


def collect_kernel(place, *refs):
    *terms, out = refs
    for by, term in enumerate(terms):
        out[lax.rem(place[3] + 4 - by, 4)] = term[...]


def collected(place, x):
    whole = pl.BlockSpec(memory_space=pltpu.VMEM)
    return pl.pallas_call(
        collect_kernel,
        in_specs=[pl.BlockSpec(memory_space=pltpu.SMEM)] + [whole] * 4,
        out_specs=whole,
        out_shape=jax.ShapeDtypeStruct((4,) + x.shape, x.dtype),
        compiler_params=pltpu.CompilerParams(vmem_limit_bytes=24 * 2**20),
        name="collected",
    )(place, *terms_along(x, "z"))


def join_kernel(place, left, *refs):
    *terms, out = refs
    for z in range(4):
        for y in range(4):
            out[z, y, :, :, :WIDE] = left[z, y]
        for by, term in enumerate(terms):
            out[z, lax.rem(place[4] + 4 - by, 4), :, :, WIDE:] = term[z]


def joined(place, left, right):
    whole = pl.BlockSpec(memory_space=pltpu.VMEM)
    return pl.pallas_call(
        join_kernel,
        in_specs=[pl.BlockSpec(memory_space=pltpu.SMEM)] + [whole] * 5,
        out_specs=whole,
        out_shape=jax.ShapeDtypeStruct((4, 4, 2, ROWS, H), bf16),
        compiler_params=pltpu.CompilerParams(vmem_limit_bytes=24 * 2**20),
        name="joined",
    )(place, left, *right)


def gathered(place, left, right):
    right = collected(place, right)
    left = exchange(left, "y")
    right, left = lax.optimization_barrier((right, left))
    right = terms_along(right, "y")
    left = exchange(repeat(left, 4), "z")
    mine = joined(place, left, right).reshape(32, ROWS, H)
    other = swap(mine, "c")
    whole = placed(place, other, 2, placed(place, mine, 1))
    return whole.reshape(1, N_DP * ROWS, H)


def shards(grad_parts, master, momentum):
    core, low = lax.axis_index("c"), lax.axis_index("xl")
    place = jnp.stack([low, core, 1 - core, lax.axis_index("z"), lax.axis_index("y")])
    place = place.astype(jnp.int32)
    shape = master.shape
    master = master.reshape(ROWS, H)
    momentum = momentum.reshape(ROWS, H)
    sums, state_other = summed_parts(place, grad_parts, jnp.concatenate([momentum, master]))
    new_momentum, direction, kept, given = direction_and_gram(
        place, *sums, momentum, state_other[:ROWS]
    )
    mine, other = summed_gram(kept, given)
    update, new_master, left, right = newton(
        place, mine, other, direction, master, state_other[ROWS:]
    )
    return (
        gathered(place, left, right),
        new_momentum.reshape(shape),
        new_master.reshape(shape),
        update.reshape(shape),
    )


def solution(mesh):
    fine = Mesh(mesh.devices.reshape(4, 4, 2, 2, 2), ("z", "y", "xl", "c", "xh"))
    rows = P(None, "xh", DP, None)
    return jax.shard_map(
        shards,
        mesh=fine,
        in_specs=(P(DP, None, "xh", None), rows, rows),
        out_specs=(P(None, "xh", None), rows, rows, rows),
        check_vma=False,
    )
```

```python
import functools

import jax
import jax.numpy as jnp
import numpy as np
from jax import lax
from jax.experimental import pallas as pl
from jax.experimental.pallas import tpu as pltpu
from jax.sharding import Mesh, PartitionSpec as P

D = 7168
H = 1024
ITERS = 3
N_DP = 64
ROWS = 56
BLOCK = 256
UPPER = [(i, j) for i in range(H // BLOCK) for j in range(i, H // BLOCK)]
PACKED = len(UPPER) * BLOCK * BLOCK // 128

beta_rate = 0.95
learn_rate = 0.02
decay_rate = 0.1
small_eps = 1e-07
coef_first = 3.4445
coef_second = -4.775
coef_third = 2.0315

f32 = jnp.float32
bf16 = jnp.bfloat16
CHIPS = ("z", "y", "xl", "xh")
DP = ("z", "y", "xl", "c")


def split(x):
    hi = x.astype(bf16)
    return hi, (x - hi.astype(f32)).astype(bf16)


def dot(a, b):
    return jnp.dot(a, b, preferred_element_type=f32)


WIDE = H // 2
QUARTER = PACKED // 4


def place_of(slab):
    return slab // 10, slab % 10 // 5, slab % 5 * BLOCK


def gram_kernel(
    place_ref, early, early_other, late, late_given, momentum, momentum_other,
    new_momentum, direction, kept, given,
):
    low = place_ref[0]

    def moved(left, right, old):
        grad = jnp.concatenate([left[...], right], axis=1)
        new = beta_rate * old[...] + grad
        return new, grad + beta_rate * new

    new, direct = moved(early, late[low] + late_given[low], momentum)
    _, direct_other = moved(early_other, late[1 - low] + late_given[1 - low], momentum_other)
    new_momentum[...] = new
    direct = jnp.concatenate([direct, direct_other], axis=0)
    direction[...] = direct
    hi, lo = split(direct)
    tall = jnp.concatenate([hi, lo, hi, lo], axis=0).T
    deep = jnp.concatenate([hi, hi, lo, lo], axis=0)
    for b, (i, j) in enumerate(UPPER):

        @pl.when(low == b // 5)
        def _():
            tile = dot(tall[i * BLOCK : (i + 1) * BLOCK], deep[:, j * BLOCK : (j + 1) * BLOCK])
            for side in range(2):
                _, core, at = place_of(2 * b + side)
                value = tile[:, side * 128 : (side + 1) * 128]

                @pl.when(place_ref[1] == core)
                def _():
                    kept[pl.ds(at, BLOCK), :] = value

                @pl.when(place_ref[1] != core)
                def _():
                    given[pl.ds(at, BLOCK), :] = value


def direction_and_gram(place, *operands):
    whole = pl.BlockSpec(memory_space=pltpu.VMEM)
    row = jax.ShapeDtypeStruct((ROWS, H), f32)
    rows = jax.ShapeDtypeStruct((2 * ROWS, H), f32)
    quarter = jax.ShapeDtypeStruct((QUARTER, 128), f32)
    return pl.pallas_call(
        gram_kernel,
        in_specs=[pl.BlockSpec(memory_space=pltpu.SMEM)] + [whole] * 6,
        out_specs=[whole] * 4,
        out_shape=[row, rows, quarter, quarter],
        compiler_params=pltpu.CompilerParams(vmem_limit_bytes=24 * 2**20),
        name="direction_and_gram",
    )(place, *operands)


def newton_kernel(
    place_ref, mine, other, direction, master, master_other,
    update, new_master, left, right, gram, g_hi, g_lo, p_hi, p_lo,
):
    n = H // BLOCK
    spans = [slice(i * BLOCK, (i + 1) * BLOCK) for i in range(n)]
    on = lax.broadcasted_iota(jnp.int32, (BLOCK, BLOCK), 0) == lax.broadcasted_iota(
        jnp.int32, (BLOCK, BLOCK), 1
    )
    first_core = place_ref[1] == 0

    def loaded(place):
        low, core, at = place_of(place // BLOCK)
        at += low * QUARTER
        a, b = mine[pl.ds(at, BLOCK), :], other[pl.ds(at, BLOCK), :]
        return jnp.where(first_core, a, b) if core == 0 else jnp.where(first_core, b, a)

    def put(value, i, j, hi_ref, lo_ref):
        hi, lo = split(value)
        hi_ref[spans[i], spans[j]] = hi
        lo_ref[spans[i], spans[j]] = lo
        if j > i:
            hi_ref[spans[j], spans[i]] = hi.T
            lo_ref[spans[j], spans[i]] = lo.T

    def full(a_hi, a_lo, b_hi, b_lo, i):
        cols = slice(i * BLOCK, H)
        b = b_hi[:, cols]
        return (
            dot(a_hi[spans[i], :], b)
            + dot(a_lo[spans[i], :], b)
            + dot(a_hi[spans[i], :], b_lo[:, cols])
        )

    def thin(x, b_hi, b_lo):
        hi, lo = split(x)
        both = dot(jnp.concatenate([hi, lo], axis=0), b_hi[...])
        return both[: 2 * ROWS] + both[2 * ROWS :] + dot(hi, b_lo[...])

    def poly():
        for i in range(n):
            square = full(g_hi, g_lo, g_hi, g_lo, i)
            for j in range(i, n):
                value = coef_second * gram[spans[i], spans[j]]
                value += coef_third * square[:, (j - i) * BLOCK : (j - i + 1) * BLOCK]
                if i == j:
                    value += jnp.where(on, coef_first, 0.0)
                put(value, i, j, p_hi, p_lo)

    def times_poly():
        for i in range(n):
            gram[spans[i], i * BLOCK :] = full(g_hi, g_lo, p_hi, p_lo, i)
        for i in range(n):
            for j in range(i, n):
                put(gram[spans[i], spans[j]], i, j, g_hi, g_lo)

    place = 0
    trace = jnp.zeros((), f32)
    for i in range(n):
        for j in range(i, n):
            tile = jnp.concatenate([loaded(place), loaded(place + BLOCK)], axis=1)
            place += 2 * BLOCK
            gram[spans[i], spans[j]] = tile
            if i == j:
                trace += jnp.sum(jnp.where(on, tile, 0.0))
    inverse = 1.0 / (jnp.sqrt(jnp.full((1, 1), trace, f32)) + small_eps)
    for i in range(n):
        for j in range(i, n):
            value = gram[spans[i], spans[j]] * inverse * inverse
            gram[spans[i], spans[j]] = value
            put(value, i, j, g_hi, g_lo)

    scaled = direction[...] * inverse
    poly()
    scaled = thin(scaled, p_hi, p_lo)
    times_poly()
    times_poly()
    poly()
    scaled = thin(scaled, p_hi, p_lo)

    def last_gram(x):
        return thin(thin(thin(x, p_hi, p_lo), p_hi, p_lo), g_hi, g_lo)

    once = last_gram(scaled)
    twice = last_gram(once)
    scaled = coef_first * scaled + coef_second * once + coef_third * twice
    result = (0.2 * max(D, H) ** 0.5) * scaled
    update[...] = result[:ROWS]

    def stepped(old, change):
        return old * (1.0 - learn_rate * decay_rate) - learn_rate * change

    moved = stepped(master[...], result[:ROWS])
    new_master[...] = moved
    weights = moved.astype(bf16)
    weights_other = stepped(master_other[...], result[ROWS:]).astype(bf16)
    low = place_ref[0]
    for at, value in ((low, weights), (1 - low, weights_other)):
        for i in range(4):
            left[i, at] = value[:, :WIDE]
        right[at] = value[:, WIDE:]


def newton(place, *operands):
    whole = pl.BlockSpec(memory_space=pltpu.VMEM)
    row = jax.ShapeDtypeStruct((ROWS, H), f32)
    return pl.pallas_call(
        newton_kernel,
        in_specs=[pl.BlockSpec(memory_space=pltpu.SMEM)] + [whole] * 5,
        out_specs=[whole] * 4,
        out_shape=[
            row,
            row,
            jax.ShapeDtypeStruct((4, 2, ROWS, WIDE), bf16),
            jax.ShapeDtypeStruct((2, ROWS, WIDE), bf16),
        ],
        scratch_shapes=[pltpu.VMEM((H, H), f32)] + [pltpu.VMEM((H, H), bf16)] * 4,
        compiler_params=pltpu.CompilerParams(vmem_limit_bytes=56 * 2**20),
        name="newton",
    )(place, *operands)


def exchange(x, axes):
    return lax.all_to_all(x, axes, 0, 0, tiled=True)


def swap(x, axis):
    return lax.ppermute(x, axis, [(0, 1), (1, 0)])


def repeat(x, n):
    return jnp.broadcast_to(x[None], (n,) + x.shape)


def pick(x, axis, index):
    return lax.dynamic_index_in_dim(x, index, axis, keepdims=False)


def late_kernel(given, grads, out, held, sems, out_sems):
    parts = [(xl, c) for xl in range(2) for c in range(2)]
    into = [
        pltpu.make_async_copy(
            grads.at[:, xl, c, :, pl.ds(WIDE, WIDE)], held.at[2 * xl + c], sems.at[2 * xl + c]
        )
        for xl, c in parts
    ]
    away = [
        pltpu.make_async_copy(held.at[2 * xl + c], out.at[:, c, xl], out_sems.at[2 * xl + c])
        for xl, c in parts
    ]
    for copy in into:
        copy.start()
    for copy, back in zip(into, away):
        copy.wait()
        back.start()
    for back in away:
        back.wait()


def late_columns(given, grads):
    return pl.pallas_call(
        late_kernel,
        in_specs=[pl.BlockSpec(memory_space=pl.ANY)] * 2,
        out_specs=pl.BlockSpec(memory_space=pltpu.HBM),
        out_shape=jax.ShapeDtypeStruct((16, 2, 2, ROWS, WIDE), bf16),
        scratch_shapes=[
            pltpu.VMEM((4, 16, ROWS, WIDE), bf16),
            pltpu.SemaphoreType.DMA((4,)),
            pltpu.SemaphoreType.DMA((4,)),
        ],
        compiler_params=pltpu.CompilerParams(vmem_limit_bytes=52 * 2**20),
        name="late_columns",
    )(given, grads)


def early_kernel(there, place, after, grads, swapped, out, held, sem):
    xl = 1 - place[0] if there else place[0]
    copy = pltpu.make_async_copy(
        grads.at[:, xl, place[1], :, pl.ds(0, WIDE)], held, sem
    )
    copy.start()
    copy.wait()
    for k in range(16):
        out[k] = held[k].astype(f32) + swapped[k, xl].astype(f32)


def early_sums(there, place, after, grads, swapped):
    whole = pl.BlockSpec(memory_space=pltpu.VMEM)
    return pl.pallas_call(
        functools.partial(early_kernel, there),
        in_specs=[
            pl.BlockSpec(memory_space=pltpu.SMEM),
            pl.BlockSpec(memory_space=pl.ANY),
            pl.BlockSpec(memory_space=pl.ANY),
            whole,
        ],
        out_specs=whole,
        out_shape=jax.ShapeDtypeStruct((16, ROWS, WIDE), f32),
        scratch_shapes=[pltpu.VMEM((16, ROWS, WIDE), bf16), pltpu.SemaphoreType.DMA],
        compiler_params=pltpu.CompilerParams(vmem_limit_bytes=16 * 2**20),
        name="early_sums",
    )(place, after, grads, swapped)


def summed_parts(place, grads, state):
    core = place[1]
    grads = grads.reshape(16, 2, 2, ROWS, H)

    def left(c):
        block = lax.dynamic_slice(grads, (0, 0, c, 0, 0), (16, 2, 1, ROWS, WIDE))
        return block.reshape(16, 2, ROWS, WIDE)

    given = left(1 - core)
    swapped = swap(given, "c")
    late = late_columns(given, grads).reshape(32, 2 * ROWS, WIDE)
    late = exchange(late, ("z", "y", "c"))
    given = early_sums(True, place, swapped, grads, swapped)
    kept = early_sums(False, place, given, grads, swapped)
    early = kept + swap(given, "xl")
    late = late.astype(f32).sum(0).reshape(2, ROWS, WIDE)
    late_given, state = lax.optimization_barrier((swap(late, "xl"), state))
    state_other = swap(state, "xl")
    early, state_other = lax.optimization_barrier((exchange(early, ("z", "y")), state_other))
    early = early.sum(0)
    return (early, swap(early, "xl"), late, late_given), state_other


def summed_gram(kept, given):
    part = kept + swap(given, "c")
    piece = exchange(part.reshape(32, -1, 128), ("z", "y", "xh")).sum(0)
    mine = exchange(repeat(piece, 64), ("xl", "z", "y", "xh")).reshape(2 * QUARTER, 128)
    return mine, swap(mine, "c")


def place_kernel(which, place, piece, *refs):
    out, sem = refs[-2:]
    copy = pltpu.make_async_copy(piece, out.at[:, place[which]], sem)
    copy.start()
    copy.wait()


def placed(place, piece, which, held=None):
    rest = [] if held is None else [held]
    return pl.pallas_call(
        functools.partial(place_kernel, which),
        in_specs=[pl.BlockSpec(memory_space=pltpu.SMEM)]
        + [pl.BlockSpec(memory_space=pltpu.VMEM)]
        + [pl.BlockSpec(memory_space=pltpu.HBM)] * len(rest),
        out_specs=pl.BlockSpec(memory_space=pltpu.HBM),
        out_shape=jax.ShapeDtypeStruct((32, 2, ROWS, H), bf16),
        input_output_aliases={2: 0} if rest else {},
        scratch_shapes=[pltpu.SemaphoreType.DMA],
        compiler_params=pltpu.CompilerParams(vmem_limit_bytes=16 * 2**20),
        name="placed",
    )(place, piece, *rest)


def terms_along(x, axis):
    return [x] + [lax.ppermute(x, axis, [(i, (i + by) % 4) for i in range(4)]) for by in (1, 2, 3)]


def collect_kernel(place, *refs):
    *terms, out = refs
    for by, term in enumerate(terms):
        out[lax.rem(place[3] + 4 - by, 4)] = term[...]


def collected(place, x):
    whole = pl.BlockSpec(memory_space=pltpu.VMEM)
    return pl.pallas_call(
        collect_kernel,
        in_specs=[pl.BlockSpec(memory_space=pltpu.SMEM)] + [whole] * 4,
        out_specs=whole,
        out_shape=jax.ShapeDtypeStruct((4,) + x.shape, x.dtype),
        compiler_params=pltpu.CompilerParams(vmem_limit_bytes=24 * 2**20),
        name="collected",
    )(place, *terms_along(x, "z"))


def join_kernel(place, left, *refs):
    *terms, out = refs
    for z in range(4):
        for y in range(4):
            out[z, y, :, :, :WIDE] = left[z, y]
        for by, term in enumerate(terms):
            out[z, lax.rem(place[4] + 4 - by, 4), :, :, WIDE:] = term[z]


def joined(place, left, right):
    whole = pl.BlockSpec(memory_space=pltpu.VMEM)
    return pl.pallas_call(
        join_kernel,
        in_specs=[pl.BlockSpec(memory_space=pltpu.SMEM)] + [whole] * 5,
        out_specs=whole,
        out_shape=jax.ShapeDtypeStruct((4, 4, 2, ROWS, H), bf16),
        compiler_params=pltpu.CompilerParams(vmem_limit_bytes=24 * 2**20),
        name="joined",
    )(place, left, *right)


def gathered(place, left, right):
    right = collected(place, right)
    left = exchange(left, "y")
    right, left = lax.optimization_barrier((right, left))
    right = terms_along(right, "y")
    left = exchange(repeat(left, 4), "z")
    mine = joined(place, left, right).reshape(32, ROWS, H)
    other = swap(mine, "c")
    whole = placed(place, other, 2, placed(place, mine, 1))
    return whole.reshape(1, N_DP * ROWS, H)


def shards(grad_parts, master, momentum):
    core, low = lax.axis_index("c"), lax.axis_index("xl")
    place = jnp.stack([low, core, 1 - core, lax.axis_index("z"), lax.axis_index("y")])
    place = place.astype(jnp.int32)
    shape = master.shape
    master = master.reshape(ROWS, H)
    momentum = momentum.reshape(ROWS, H)
    sums, state_other = summed_parts(place, grad_parts, jnp.concatenate([momentum, master]))
    new_momentum, direction, kept, given = direction_and_gram(
        place, *sums, momentum, state_other[:ROWS]
    )
    mine, other = summed_gram(kept, given)
    update, new_master, left, right = newton(
        place, mine, other, direction, master, state_other[ROWS:]
    )
    return (
        gathered(place, left, right),
        new_momentum.reshape(shape),
        new_master.reshape(shape),
        update.reshape(shape),
    )


def solution(mesh):
    fine = Mesh(mesh.devices.reshape(4, 4, 2, 2, 2), ("z", "y", "xl", "c", "xh"))
    rows = P(None, "xh", DP, None)
    return jax.shard_map(
        shards,
        mesh=fine,
        in_specs=(P(DP, None, "xh", None), rows, rows),
        out_specs=(P(None, "xh", None), rows, rows, rows),
        check_vma=False,
    )
```
